32 devices in a mesh: seq: 4 (over y, x), res: 8 (over z, core).
Axes of the slice: x: 2, y: 2, z: 4, core: 2. Of those that a mesh axis runs over, the one named last changes fastest.
Arguments:
- homolog_features: bfloat16 [512, 128, 256], P('seq', 'res')
- standardize_scale: float32 [256], replicated, may hold values from 0.25 to 1.75
- left_factor_matrix: bfloat16 [256, 32], replicated, may hold values from -0.375 to 0.375
- right_factor_matrix: bfloat16 [256, 32], replicated, may hold values from -0.375 to 0.375
- final_mapping_matrix: bfloat16 [1024, 128], replicated, may hold values from -0.1875 to 0.1875
- final_offset_entries: float32 [128], replicated, may hold values from -2 to 2
- incoming_sensitivity: bfloat16 [128, 128, 128], P('res', 'seq'), may hold values from -48 to 48
Outputs:
- pair_delta_update: bfloat16 [128, 128, 128], P('res', 'seq')
- activation_cotangent: bfloat16 [512, 128, 256], P('seq', 'res')
The draws below stay inside these ranges and needn't reach their ends.
All inputs are finite; a program needn't handle non-finite values.
Results may differ from the reference program's by a relative error of at most 0.009.
Values may be sent and summed in bfloat16 or wider, within the bound.
A program may use at most 192 MiB of HBM per device.

```python
import jax
import jax.numpy as jnp
from jax import lax

FEATURE_COUNT = 256
PROJ_WIDTH = 32
CZ = 128
RES_DEV = 16
HOMOLOG_COUNT = 512
CROP_LENGTH = 128


def draw_homolog_features(key, part):
    key = jax.random.fold_in(key, 11)
    common_random_seed, random_perturb_seed = jax.random.split(key, 2)
    common_draw = jax.random.normal(common_random_seed, (1, CROP_LENGTH, FEATURE_COUNT), jnp.float32)
    random_perturbation = jax.random.normal(random_perturb_seed, (HOMOLOG_COUNT, CROP_LENGTH, FEATURE_COUNT), jnp.float32)
    values = common_draw + random_perturbation
    return values.astype(jnp.bfloat16)


def block_scale(stream_key, shape, cuts, smallest, top_value):
    loudness, own = 1.0, jax.random.fold_in(stream_key, 6)
    for axis_at, shards_of in cuts:
        draws = jnp.exp(jax.random.uniform(jax.random.fold_in(own, axis_at), (shards_of,), jnp.float32, smallest / len(cuts), top_value / len(cuts)))
        loudness = loudness * jnp.repeat(draws, shape[axis_at] // shards_of).reshape([-1 if axis == axis_at else 1 for axis in range(len(shape))])
    return loudness


def gaussian(stream_key, shape, deviation, reach, shards=(), kind=jnp.bfloat16):
    level = block_scale(stream_key, shape, shards, -0.22, 0.18) if shards else 1.0
    array = jax.random.normal(stream_key, shape, jnp.float32) * deviation * level
    return jnp.minimum(jnp.maximum(array, -reach), reach).astype(kind)


def setup_inputs(seed: int = 0) -> dict:
    arg_keys = jax.random.split(jax.random.key(seed), 8)
    homolog_features = draw_homolog_features(jax.random.fold_in(arg_keys[7], 71), 0)
    standardize_scale = jnp.clip(1.0 + 0.15 * jax.random.normal(arg_keys[1], (FEATURE_COUNT,), jnp.float32), 0.25, 1.75)
    left_factor_matrix = gaussian(arg_keys[2], (FEATURE_COUNT, PROJ_WIDTH), FEATURE_COUNT ** -0.5, 0.375)
    right_factor_matrix = gaussian(arg_keys[3], (FEATURE_COUNT, PROJ_WIDTH), FEATURE_COUNT ** -0.5, 0.375)
    final_mapping_matrix = gaussian(arg_keys[4], (PROJ_WIDTH * PROJ_WIDTH, CZ), (PROJ_WIDTH * PROJ_WIDTH) ** -0.5, 0.1875)
    final_offset_entries = gaussian(arg_keys[5], (CZ,), 0.3, 2.0, (), jnp.float32)
    incoming_sensitivity = gaussian(arg_keys[6], (CROP_LENGTH, CROP_LENGTH, CZ), 8.0, 48.0, ((0, 8), (1, 4)))
    return {"homolog_features": homolog_features, "standardize_scale": standardize_scale, "left_factor_matrix": left_factor_matrix, "right_factor_matrix": right_factor_matrix, "final_mapping_matrix": final_mapping_matrix, "final_offset_entries": final_offset_entries, "incoming_sensitivity": incoming_sensitivity}


def standardizer_apply(values, standardize_scale):
    mean = lax.optimization_barrier(jnp.mean(values, axis=-1, keepdims=True))
    centred = values - mean
    variance = lax.optimization_barrier(jnp.mean(centred * centred, axis=-1, keepdims=True))
    return centred * lax.rsqrt(variance + 1e-05) * standardize_scale

def reference(homolog_features, standardize_scale, left_factor_matrix, right_factor_matrix, final_mapping_matrix, final_offset_entries, incoming_sensitivity):
    homolog_number = homolog_features.shape[0]
    position_number = homolog_features.shape[1]
    standardized_features, standardizer_adjoint = jax.vjp(lambda spread_moment: standardizer_apply(spread_moment, standardize_scale), homolog_features.astype(jnp.float32))
    centered_scaled_part = standardized_features.astype(jnp.bfloat16).reshape(homolog_number * position_number, FEATURE_COUNT)
    left = jnp.dot(centered_scaled_part, left_factor_matrix, preferred_element_type=jnp.float32).astype(jnp.bfloat16).reshape(homolog_number, position_number, PROJ_WIDTH)
    right = jnp.dot(centered_scaled_part, right_factor_matrix, preferred_element_type=jnp.float32).astype(jnp.bfloat16).reshape(homolog_number, position_number, PROJ_WIDTH)
    left32 = left.astype(jnp.float32)
    right32 = right.astype(jnp.float32)
    out_w32 = final_mapping_matrix.astype(jnp.float32)
    blocks = position_number // RES_DEV
    scale = jnp.float32(1.0) / jnp.float32(homolog_number)

    def one_block(grad_right, index):
        start = (index * RES_DEV).astype(jnp.int32)
        rows_left = lax.dynamic_slice_in_dim(left32, start, RES_DEV, 1)
        outer = jnp.einsum('sic,sjd->ijcd', rows_left, right32) * scale
        pair = jnp.dot(outer.reshape(RES_DEV * position_number, PROJ_WIDTH * PROJ_WIDTH), out_w32, precision=lax.Precision.HIGHEST) + final_offset_entries
        pair = pair.astype(jnp.bfloat16).reshape(RES_DEV, position_number, CZ)
        cot_rows = lax.dynamic_slice_in_dim(incoming_sensitivity, start, RES_DEV, 0).reshape(RES_DEV * position_number, CZ)
        d_outer = lax.dot_general(cot_rows, final_mapping_matrix, (((1,), (1,)), ((), ())), preferred_element_type=jnp.float32)
        d_outer = d_outer.astype(jnp.bfloat16).astype(jnp.float32).reshape(RES_DEV, position_number, PROJ_WIDTH, PROJ_WIDTH)
        grad_left = jnp.einsum('ijcd,sjd->sic', d_outer, right32) * scale
        grad_right = grad_right + jnp.einsum('ijcd,sic->sjd', d_outer, rows_left)
        return (grad_right, (pair, grad_left.astype(jnp.bfloat16)))
    init = jnp.zeros((homolog_number, position_number, PROJ_WIDTH), jnp.float32)
    grad_right, (pairs, grad_lefts) = lax.scan(one_block, init, jnp.arange(blocks, dtype=jnp.int32))
    pair_delta_update = pairs.reshape(position_number, position_number, CZ)
    grad_left = jnp.transpose(grad_lefts, (1, 0, 2, 3)).reshape(homolog_number * position_number, PROJ_WIDTH)
    grad_right = (grad_right * scale).astype(jnp.bfloat16).reshape(homolog_number * position_number, PROJ_WIDTH)
    standardized_sensitivity = lax.dot_general(grad_left, left_factor_matrix, (((1,), (1,)), ((), ())), preferred_element_type=jnp.float32)
    standardized_sensitivity = standardized_sensitivity + lax.dot_general(grad_right, right_factor_matrix, (((1,), (1,)), ((), ())), preferred_element_type=jnp.float32)
    activation_cotangent = standardizer_adjoint(standardized_sensitivity.reshape(homolog_number, position_number, FEATURE_COUNT))[0].astype(jnp.bfloat16)
    return (pair_delta_update, activation_cotangent)
```

```python
import functools

import jax
import jax.numpy as jnp
from jax import lax
from jax.experimental import pallas as pl
from jax.experimental.pallas import tpu as pltpu
from jax.sharding import PartitionSpec as P

MESH = pl.DeviceIdType.MESH
F32, BF16 = jnp.float32, jnp.bfloat16
NT = (((1,), (1,)), ((), ()))
TN = (((0,), (0,)), ((), ()))
VMEM = pltpu.VMEM
LIMIT = 48 * 1024 * 1024


def moments(x):
    mean = jnp.mean(x, axis=-1, keepdims=True)
    centred = x - mean
    variance = jnp.mean(centred * centred, axis=-1, keepdims=True)
    rstd = lax.rsqrt(variance + 1e-05)
    return centred * rstd, rstd


def lane_group(shape, width, groups, axis):
    index = lax.broadcasted_iota(jnp.int32, shape, axis)
    return lax.rem(lax.div(index, width), groups)


def project_kernel(x_ref, gain_ref, w_ref, left_ref, right_ref):
    feats, width = w_ref.shape
    half = width // 2
    chan = half // 4
    gain = gain_ref[...]
    w = w_ref[...]
    group = lane_group(w.shape, chan, 4, 1)
    parts = [jnp.where(group == m, w, jnp.zeros_like(w)) for m in range(4)]
    residues = x_ref.shape[1] // feats
    for quad in range(residues // 4):
        acc = jnp.zeros((x_ref.shape[0], width), F32)
        for m in range(4):
            i = quad * 4 + m
            hat, _ = moments(x_ref[:, i * feats : (i + 1) * feats].astype(F32))
            normed = (hat * gain).astype(BF16)
            acc += jnp.dot(normed, parts[m], preferred_element_type=F32)
        left_ref[:, quad * half : (quad + 1) * half] = acc[:, :half].astype(BF16)
        right_ref[:, quad * half : (quad + 1) * half] = acc[:, half:].astype(BF16)


def place(nq):
    q = lax.axis_index("seq")
    r = lax.axis_index("res")
    return q, r // 2, lax.rem(r, 2)


def greet(nq, q, g, h):
    barrier = pltpu.get_barrier_semaphore()
    peers = [(q, 2 * g + 1 - h)]
    for o in range(1, nq):
        peers.append((lax.rem(q + o, nq), 2 * g + h))
        peers.append((q, 2 * lax.rem(g + o, nq) + h))
    for peer in peers:
        pl.semaphore_signal(barrier, inc=1, device_id=peer, device_id_type=MESH)
    pl.semaphore_wait(barrier, len(peers))


def send(src, dst, send_sem, recv_sem, device):
    return pltpu.make_async_remote_copy(
        src_ref=src, dst_ref=dst, send_sem=send_sem, recv_sem=recv_sem,
        device_id=device, device_id_type=MESH,
    )


def gather_kernel(nq, left_ref, right_ref, la_ref, rt_ref, zbuf, ss, rs, zss, zrs, pss, prs, css, crs):
    q, g, h = place(nq)
    me = 2 * g + h
    greet(nq, q, g, h)
    zs, ls = [], []
    for o in range(1, nq):
        to = 2 * lax.rem(g + o, nq) + h
        c = send(right_ref, zbuf.at[g], zss.at[o], zrs.at[o], (q, to))
        c.start()
        zs.append(c)
    for o in range(1, nq):
        c = send(left_ref, la_ref.at[q], ss.at[o], rs.at[o], (lax.rem(q + o, nq), me))
        c.start()
        ls.append(c)
    la_ref[q] = left_ref[...]

    def forward(o, src, g2):
        @pl.when(g2 != q)
        def _():
            send(src, rt_ref.at[h, q], pss.at[o], prs.at[q], (g2, me)).start()

        @pl.when(g2 == q)
        def _():
            rt_ref[h, q] = src[...]

    forward(0, right_ref, g)
    for o in range(1, nq):
        g2 = lax.rem(g + nq - o, nq)
        send(right_ref, zbuf.at[g2], zss.at[o], zrs.at[o], (q, me)).wait_recv()
        forward(o, zbuf.at[g2], g2)
    cs = []
    for p in range(nq):
        src = lax.rem(q + nq - p, nq)
        if p:
            send(right_ref, rt_ref.at[h, src], pss.at[0], prs.at[src], (q, me)).wait_recv()
        c = send(rt_ref.at[h, src], rt_ref.at[h, src], css.at[p], crs.at[p], (q, 2 * g + 1 - h))
        c.start()
        cs.append(c)
    for p in range(nq):
        src = lax.rem(q + nq - p, nq)
        send(rt_ref.at[h, src], rt_ref.at[1 - h, src], css.at[p], crs.at[p], (q, me)).wait_recv()
    for o in range(1, nq):
        src = lax.rem(q + nq - o, nq)
        send(left_ref, la_ref.at[src], ss.at[o], rs.at[o], (q, me)).wait_recv()
    for c in cs + zs + ls:
        c.wait_send()
    for o in range(nq):
        g2 = lax.rem(g + nq - o, nq)

        @pl.when(g2 != q)
        def _():
            send(right_ref, rt_ref.at[h, q], pss.at[o], prs.at[q], (g2, me)).wait_send()


def scatter_kernel(nq, glp_ref, grp_ref, gl_ref, gr_ref, glr, cbuf, sums, pbuf, zb,
                   ss, rs, css, crs, pss, prs, zss, zrs):
    q, g, h = place(nq)
    me = 2 * g + h
    other = (q, 2 * g + 1 - h)
    greet(nq, q, g, h)
    cs, ls, ps = [], [], []
    for p in range(nq):
        to = lax.rem(q + p + 1, nq)
        c = send(grp_ref.at[1 - h, to], cbuf.at[to], css.at[p], crs.at[p], other)
        c.start()
        cs.append(c)
    for o in range(1, nq):
        to = lax.rem(q + o, nq)
        c = send(glp_ref.at[to], glr.at[q], ss.at[o], rs.at[o], (to, me))
        c.start()
        ls.append(c)
    glr[q] = glp_ref[q]
    for p in range(nq):
        to = lax.rem(q + p + 1, nq)
        cs[p].wait_recv()
        total = (cbuf[to].astype(F32) + grp_ref[h, to].astype(F32)).astype(BF16)
        sums[to] = total
        if p < nq - 1:
            c = send(sums.at[to], pbuf.at[q], pss.at[p + 1], prs.at[p + 1], (to, me))
            c.start()
            ps.append(c)

    def forward(o, ref, src):
        @pl.when(src != g)
        def _():
            send(ref, zb.at[g], zss.at[o], zrs.at[g], (q, 2 * src + h)).start()

        @pl.when(src == g)
        def _():
            zb[g] = ref[...]

    forward(0, sums.at[q], q)
    for o in range(1, nq):
        src = lax.rem(q + nq - o, nq)
        send(sums.at[src], pbuf.at[src], pss.at[o], prs.at[o], (q, me)).wait_recv()
        forward(o, pbuf.at[src], src)
    for o in range(1, nq):
        src = lax.rem(q + nq - o, nq)
        send(glp_ref.at[src], glr.at[src], ss.at[o], rs.at[o], (q, me)).wait_recv()
    scale = F32(1.0 / (nq * gl_ref.shape[0]))
    total = glr[0].astype(F32)
    for p in range(1, nq):
        total += glr[p].astype(F32)
    gl_ref[...] = (total * scale).astype(BF16)
    for p in range(1, nq):
        src = lax.rem(g + p, nq)
        send(pbuf.at[0], zb.at[src], zss.at[0], zrs.at[src], (q, me)).wait_recv()
    total = zb[0].astype(F32)
    for p in range(1, nq):
        total += zb[p].astype(F32)
    gr_ref[...] = (total * scale).astype(BF16)
    for c in cs + ls + ps:
        c.wait_send()
    for o in range(nq):
        src = lax.rem(q + nq - o, nq)

        @pl.when(src != g)
        def _():
            send(pbuf.at[0], zb.at[g], zss.at[o], zrs.at[g], (q, 2 * src + h)).wait_send()


def weight_block(wrep_ref, k, chan):
    wide = 8 * chan
    w = wrep_ref[:, pl.ds(pl.multiple_of(k * wide, wide), wide)]
    group = lane_group(w.shape, chan, 4, 1)
    return jnp.concatenate([jnp.where(group == m, w, jnp.zeros_like(w)) for m in range(4)], axis=0)


def cotangent_kernel(chan, cot_ref, wrep_ref, d_ref, big):
    lanes = big.shape[1]
    quads = d_ref.shape[1] // lanes
    high = big.shape[0] // quads
    rows = high // chan

    def step(k, _):
        out = jnp.dot(cot_ref[...], weight_block(wrep_ref, k, chan), preferred_element_type=F32)
        for a in range(2):
            for b in range(quads):
                big[pl.ds(b * high + 2 * k + a, rows, stride=chan), :] = out[
                    b * rows : (b + 1) * rows, a * lanes : (a + 1) * lanes
                ]
        return 0

    lax.fori_loop(0, chan // 2, step, 0)
    for b in range(quads):
        d_ref[:, b * lanes : (b + 1) * lanes] = big[b * high : (b + 1) * high, :].astype(BF16)


def partial_kernel(nq, la_ref, rt_ref, d_ref, glp_ref, grp_ref):
    half = rt_ref.shape[3]

    def step(t, _):
        left = la_ref[t]
        acc = None
        for a in range(2):
            d = d_ref[:, a * half : (a + 1) * half]
            grp_ref[a, t] = jnp.dot(left, d, preferred_element_type=F32).astype(BF16)
            term = lax.dot_general(rt_ref[a, t], d, NT, preferred_element_type=F32)
            acc = term if acc is None else acc + term
        glp_ref[t] = acc.astype(BF16)
        return 0

    lax.fori_loop(0, nq, step, 0)


def pair_kernel(nq, chan, la_ref, rt_ref, wrep_ref, bias_ref, out_ref, big):
    seqs, half = la_ref.shape[1], rt_ref.shape[3]
    lanes = big.shape[1]
    quads = 2 * half // lanes
    high = big.shape[0] // quads
    rows = high // chan
    left = la_ref[...].reshape(nq * seqs, la_ref.shape[2])
    for a in range(2):
        right = rt_ref[a].reshape(nq * seqs, half)
        outer = lax.dot_general(left, right, TN, preferred_element_type=F32)
        for b in range(quads // 2):
            start = (a * (quads // 2) + b) * high
            big[start : start + high, :] = outer[:, b * lanes : (b + 1) * lanes]

    def step(k, acc):
        lhs = jnp.concatenate(
            [
                jnp.concatenate(
                    [
                        big[pl.ds(b * high + 2 * k + a, rows, stride=chan), :]
                        for b in range(quads)
                    ],
                    axis=0,
                )
                for a in range(2)
            ],
            axis=1,
        ).astype(BF16)
        return acc + lax.dot_general(lhs, weight_block(wrep_ref, k, chan), NT, preferred_element_type=F32)

    acc = lax.fori_loop(0, chan // 2, step, jnp.zeros(out_ref.shape, F32))
    scale = F32(1.0 / (nq * seqs))
    out_ref[...] = (acc * scale + bias_ref[...]).astype(BF16)


def adjoint_kernel(x_ref, gain_ref, w_ref, gl_ref, gr_ref, out_ref):
    feats, width = w_ref.shape
    half = width // 2
    chan = half // 4
    gain = gain_ref[...]
    w = w_ref[...]
    group = lane_group(w.shape, chan, 4, 1)
    parts = [jnp.where(group == m, w, jnp.zeros_like(w)) for m in range(4)]
    residues = x_ref.shape[1] // feats
    for quad in range(residues // 4):
        cols = slice(quad * half, (quad + 1) * half)
        grads = jnp.concatenate([gl_ref[:, cols], gr_ref[:, cols]], axis=1)
        for m in range(4):
            i = quad * 4 + m
            hat, rstd = moments(x_ref[:, i * feats : (i + 1) * feats].astype(F32))
            dy = lax.dot_general(grads, parts[m], NT, preferred_element_type=F32) * gain
            mean = jnp.mean(dy, axis=-1, keepdims=True)
            proj = jnp.mean(dy * hat, axis=-1, keepdims=True)
            out_ref[:, i * feats : (i + 1) * feats] = (rstd * (dy - mean - hat * proj)).astype(BF16)


def local(
    homolog_features,
    standardize_scale,
    left_factor_matrix,
    right_factor_matrix,
    final_mapping_matrix,
    final_offset_entries,
    incoming_sensitivity,
):
    seqs, residues, feats = homolog_features.shape
    chan = left_factor_matrix.shape[1]
    zdim = final_mapping_matrix.shape[1]
    cols = incoming_sensitivity.shape[1]
    nq = lax.axis_size("seq")
    wide = residues * chan
    params = pltpu.CompilerParams(vmem_limit_bytes=LIMIT)

    def remote(number):
        return pltpu.CompilerParams(vmem_limit_bytes=LIMIT, collective_id=number, has_side_effects=True)

    def sds(*shape):
        return jax.ShapeDtypeStruct(shape, BF16)

    x = homolog_features.reshape(seqs, residues * feats)
    gain = standardize_scale.reshape(1, feats)
    w4 = jnp.concatenate([jnp.tile(left_factor_matrix, (1, 4)), jnp.tile(right_factor_matrix, (1, 4))], axis=1)
    wrep = jnp.transpose(final_mapping_matrix).reshape(zdim, chan, 1, chan)
    wrep = jnp.broadcast_to(wrep, (zdim, chan, 4, chan)).reshape(zdim, 4 * chan * chan)
    cot = incoming_sensitivity.reshape(residues, cols // 4, 4, zdim)
    cot = jnp.transpose(cot, (1, 0, 2, 3)).reshape(cols // 4 * residues, 4 * zdim)
    bias = jnp.tile(final_offset_entries, 4).reshape(1, 4 * zdim)
    dma = pltpu.SemaphoreType.DMA((nq,))

    left, right = pl.pallas_call(
        project_kernel, out_shape=[sds(seqs, wide)] * 2, compiler_params=params, name="project"
    )(x, gain, w4)
    la, rt = pl.pallas_call(
        functools.partial(gather_kernel, nq),
        out_shape=[sds(nq, seqs, wide), sds(2, nq, seqs, wide)],
        in_specs=[pl.BlockSpec(memory_space=VMEM)] * 2,
        out_specs=[pl.BlockSpec(memory_space=VMEM)] * 2,
        scratch_shapes=[VMEM((nq, seqs, wide), BF16)] + [dma] * 8,
        compiler_params=remote(0),
        name="gather",
    )(left, right)
    d = pl.pallas_call(
        functools.partial(cotangent_kernel, chan),
        out_shape=sds(wide, cols * chan),
        scratch_shapes=[VMEM((cols // 4 * wide, 4 * chan), F32)],
        compiler_params=params,
        name="cotangent",
    )(cot, wrep)
    glp, grp = pl.pallas_call(
        functools.partial(partial_kernel, nq),
        out_shape=[sds(nq, seqs, wide), sds(2, nq, seqs, wide)],
        compiler_params=params,
        name="partial",
    )(la, rt, d)
    gl, gr = pl.pallas_call(
        functools.partial(scatter_kernel, nq),
        out_shape=[sds(seqs, wide)] * 2,
        in_specs=[pl.BlockSpec(memory_space=VMEM)] * 2,
        out_specs=[pl.BlockSpec(memory_space=VMEM)] * 2,
        scratch_shapes=[VMEM((nq, seqs, wide), BF16)] * 5 + [dma] * 8,
        compiler_params=remote(1),
        name="scatter",
    )(glp, grp)
    pair = pl.pallas_call(
        functools.partial(pair_kernel, nq, chan),
        out_shape=sds(cols // 4 * residues, 4 * zdim),
        scratch_shapes=[VMEM((cols // 4 * wide, 4 * chan), F32)],
        compiler_params=params,
        name="pair",
    )(la, rt, wrep, bias)
    out = pl.pallas_call(
        adjoint_kernel, out_shape=sds(seqs, residues * feats), compiler_params=params, name="adjoint"
    )(x, gain, w4, gl, gr)
    pair = jnp.transpose(pair.reshape(cols // 4, residues, 4, zdim), (1, 0, 2, 3))
    return pair.reshape(residues, cols, zdim), out.reshape(seqs, residues, feats)


def solution(mesh):
    placed = (P("seq", "res", None), P(), P(), P(), P(), P(), P("res", "seq", None))
    return jax.shard_map(
        local,
        mesh=mesh,
        in_specs=placed,
        out_specs=(P("res", "seq", None), P("seq", "res", None)),
        check_vma=False,
    )
```

```python
import functools

import jax
import jax.numpy as jnp
from jax import lax
from jax.experimental import pallas as pl
from jax.experimental.pallas import tpu as pltpu
from jax.sharding import PartitionSpec as P

MESH = pl.DeviceIdType.MESH
F32, BF16 = jnp.float32, jnp.bfloat16
NT = (((1,), (1,)), ((), ()))
TN = (((0,), (0,)), ((), ()))
VMEM = pltpu.VMEM
LIMIT = 48 * 1024 * 1024


def moments(x):
    mean = jnp.mean(x, axis=-1, keepdims=True)
    centred = x - mean
    variance = jnp.mean(centred * centred, axis=-1, keepdims=True)
    rstd = lax.rsqrt(variance + 1e-05)
    return centred * rstd, rstd


def lane_group(shape, width, groups, axis):
    index = lax.broadcasted_iota(jnp.int32, shape, axis)
    return lax.rem(lax.div(index, width), groups)


def place(nq):
    q = lax.axis_index("seq")
    r = lax.axis_index("res")
    return q, r // 2, lax.rem(r, 2)


def greet(nq, q, g, h):
    barrier = pltpu.get_barrier_semaphore()
    peers = [(q, 2 * g + 1 - h)]
    for o in range(1, nq):
        peers.append((lax.rem(q + o, nq), 2 * g + h))
        peers.append((q, 2 * lax.rem(g + o, nq) + h))
    for peer in peers:
        pl.semaphore_signal(barrier, inc=1, device_id=peer, device_id_type=MESH)
    return barrier, len(peers)


def send(src, dst, send_sem, recv_sem, device):
    return pltpu.make_async_remote_copy(
        src_ref=src, dst_ref=dst, send_sem=send_sem, recv_sem=recv_sem,
        device_id=device, device_id_type=MESH,
    )


def masked_parts(w_ref):
    w = w_ref[...]
    group = lane_group(w.shape, w.shape[1] // 8, 4, 1)
    return [jnp.where(group == m, w, jnp.zeros_like(w)) for m in range(4)]


def project(x_ref, gain_ref, w_ref, left_ref, right_ref):
    feats, width = w_ref.shape
    half = width // 2
    gain = gain_ref[...]
    parts = masked_parts(w_ref)
    residues = x_ref.shape[1] // feats
    for quad in range(residues // 4):
        acc = jnp.zeros((x_ref.shape[0], width), F32)
        for m in range(4):
            i = quad * 4 + m
            hat, _ = moments(x_ref[:, i * feats : (i + 1) * feats].astype(F32))
            normed = (hat * gain).astype(BF16)
            acc += jnp.dot(normed, parts[m], preferred_element_type=F32)
        left_ref[:, quad * half : (quad + 1) * half] = acc[:, :half].astype(BF16)
        right_ref[:, quad * half : (quad + 1) * half] = acc[:, half:].astype(BF16)


def weight_block(map_ref, k, chan):
    rows = []
    for a in range(2):
        w = map_ref[pl.ds(pl.multiple_of((2 * k + a) * chan, chan), chan), :]
        zero = jnp.zeros_like(w)
        for m in range(4):
            rows.append(jnp.concatenate([w if n == m else zero for n in range(4)], axis=1))
    return jnp.concatenate(rows, axis=0)


def cotangent(chan, cot_ref, map_ref, flat, big, d_ref):
    lanes = big.shape[1]
    quads = 2 * d_ref.shape[2] // lanes
    high = big.shape[0] // quads
    rows = high // chan
    cols = 4 * quads
    flat[...] = cot_ref[...].astype(F32)
    cot = jnp.concatenate(
        [
            jnp.concatenate(
                [flat[pl.ds(4 * b + m, rows, stride=cols), :].astype(BF16) for m in range(4)], axis=1
            )
            for b in range(quads)
        ],
        axis=0,
    )

    def step(k, _):
        out = lax.dot_general(cot, weight_block(map_ref, k, chan), NT, preferred_element_type=F32)
        for a in range(2):
            for b in range(quads):
                big[pl.ds(b * high + 2 * k + a, rows, stride=chan), :] = out[
                    b * rows : (b + 1) * rows, a * lanes : (a + 1) * lanes
                ]
        return 0

    lax.fori_loop(0, chan // 2, step, 0)
    for b in range(quads):
        at = b % (quads // 2) * lanes
        d_ref[b // (quads // 2), :, at : at + lanes] = big[b * high : (b + 1) * high, :].astype(BF16)


def pair_update(nq, chan, la_ref, rt_ref, map_ref, bias_ref, out_ref, flat, big):
    seqs, half = la_ref.shape[1], rt_ref.shape[3]
    lanes = big.shape[1]
    quads = 2 * half // lanes
    high = big.shape[0] // quads
    rows = high // chan
    left = la_ref[...].reshape(nq * seqs, la_ref.shape[2])
    for a in range(2):
        right = rt_ref[a].reshape(nq * seqs, half)
        outer = lax.dot_general(left, right, TN, preferred_element_type=F32)
        for b in range(quads // 2):
            start = (a * (quads // 2) + b) * high
            big[start : start + high, :] = outer[:, b * lanes : (b + 1) * lanes]

    def step(k, acc):
        lhs = jnp.concatenate(
            [
                jnp.concatenate(
                    [big[pl.ds(b * high + 2 * k + a, rows, stride=chan), :] for b in range(quads)], axis=0
                )
                for a in range(2)
            ],
            axis=1,
        ).astype(BF16)
        return acc + jnp.dot(lhs, weight_block(map_ref, k, chan), preferred_element_type=F32)

    zdim = map_ref.shape[1]
    acc = lax.fori_loop(0, chan // 2, step, jnp.zeros((quads * rows, 4 * zdim), F32))
    scale = F32(1.0 / (nq * seqs))
    for b in range(quads):
        for m in range(4):
            flat[pl.ds(4 * b + m, rows, stride=4 * quads), :] = (
                acc[b * rows : (b + 1) * rows, m * zdim : (m + 1) * zdim] * scale + bias_ref[...]
            )
    out_ref[...] = flat[...].astype(BF16)


def adjoint(x_ref, gain_ref, w_ref, gl, gr, out_ref):
    feats, width = w_ref.shape
    half = width // 2
    gain = gain_ref[...]
    parts = masked_parts(w_ref)
    residues = x_ref.shape[1] // feats
    for quad in range(residues // 4):
        cols = slice(quad * half, (quad + 1) * half)
        grads = jnp.concatenate([gl[:, cols], gr[:, cols]], axis=1)
        for m in range(4):
            i = quad * 4 + m
            hat, rstd = moments(x_ref[:, i * feats : (i + 1) * feats].astype(F32))
            dy = lax.dot_general(grads, parts[m], NT, preferred_element_type=F32) * gain
            mean = jnp.mean(dy, axis=-1, keepdims=True)
            proj = jnp.mean(dy * hat, axis=-1, keepdims=True)
            out_ref[:, i * feats : (i + 1) * feats] = (rstd * (dy - mean - hat * proj)).astype(BF16)


def kernel(
    nq, chan, x_ref, gain_ref, w_ref, map_ref, bias_ref, cot_ref, pair_ref, out_ref,
    left, right, la, rt, zbuf, flat, big, d, glp, grp, cbuf, sums, pbuf, zb, glr,
    ls, lr, zs, zr, ps, pr, cs, cr, gcs, gcr, gps, gpr, gzs, gzr, ss, rs,
):
    q, g, h = place(nq)
    me = 2 * g + h
    here = (q, me)
    other = (q, 2 * g + 1 - h)
    barrier, peers = greet(nq, q, g, h)
    project(x_ref, gain_ref, w_ref, left, right)
    pl.semaphore_wait(barrier, peers)
    sent = []

    def start(*args):
        copy = send(*args)
        copy.start()
        sent.append(copy)

    for o in range(1, nq):
        start(left, la.at[q], ls.at[o], lr.at[o], (lax.rem(q + o, nq), me))
    for o in range(1, nq):
        start(right, zbuf.at[g], zs.at[o], zr.at[o], (q, 2 * lax.rem(g + o, nq) + h))
    la[q] = left[...]

    cotangent(chan, cot_ref, map_ref, flat, big, d)

    for o in range(1, nq):
        src = lax.rem(q + nq - o, nq)
        send(left, la.at[src], ls.at[o], lr.at[o], here).wait_recv()

    for p in range(nq):
        to = lax.rem(q + p + 1, nq)
        grp[to] = jnp.dot(la[to], d[1 - h], preferred_element_type=F32).astype(BF16)
        start(grp.at[to], cbuf.at[to], gcs.at[p], gcr.at[p], other)
    for p in range(nq):
        to = lax.rem(q + p + 1, nq)
        total = jnp.dot(la[to], d[h], preferred_element_type=F32)
        send(grp.at[to], cbuf.at[to], gcs.at[p], gcr.at[p], here).wait_recv()
        sums[to] = (total + cbuf[to].astype(F32)).astype(BF16)
        if p < nq - 1:
            start(sums.at[to], pbuf.at[q], gps.at[p + 1], gpr.at[p + 1], (to, me))

    def forward_right(o, src, g2):
        @pl.when(g2 != q)
        def _():
            send(src, rt.at[h, q], ps.at[o], pr.at[q], (g2, me)).start()

        @pl.when(g2 == q)
        def _():
            rt[h, q] = src[...]

    forward_right(0, right, g)
    for o in range(1, nq):
        g2 = lax.rem(g + nq - o, nq)
        send(right, zbuf.at[g2], zs.at[o], zr.at[o], here).wait_recv()
        forward_right(o, zbuf.at[g2], g2)

    def forward_grad(o, ref, src):
        @pl.when(src != g)
        def _():
            send(ref, zb.at[g], gzs.at[o], gzr.at[g], (q, 2 * src + h)).start()

        @pl.when(src == g)
        def _():
            zb[g] = ref[...]

    forward_grad(0, sums.at[q], q)
    for o in range(1, nq):
        src = lax.rem(q + nq - o, nq)
        send(sums.at[src], pbuf.at[src], gps.at[o], gpr.at[o], here).wait_recv()
        forward_grad(o, pbuf.at[src], src)

    for p in range(nq):
        src = lax.rem(q + nq - p, nq)
        if p:
            send(right, rt.at[h, src], ps.at[0], pr.at[src], here).wait_recv()
        start(rt.at[h, src], rt.at[h, src], cs.at[p], cr.at[p], other)
    for p in range(nq):
        src = lax.rem(q + nq - p, nq)
        send(rt.at[h, src], rt.at[1 - h, src], cs.at[p], cr.at[p], here).wait_recv()

    for p in range(nq):
        to = lax.rem(q + p + 1, nq)
        term = lax.dot_general(rt[0, to], d[0], NT, preferred_element_type=F32)
        term += lax.dot_general(rt[1, to], d[1], NT, preferred_element_type=F32)
        glp[to] = term.astype(BF16)
        if p < nq - 1:
            start(glp.at[to], glr.at[q], ss.at[p + 1], rs.at[p + 1], (to, me))
    glr[q] = glp[q]

    pair_update(nq, chan, la, rt, map_ref, bias_ref, pair_ref, flat, big)

    for o in range(1, nq):
        src = lax.rem(q + nq - o, nq)
        send(glp.at[src], glr.at[src], ss.at[o], rs.at[o], here).wait_recv()
    for p in range(1, nq):
        src = lax.rem(g + p, nq)
        send(pbuf.at[0], zb.at[src], gzs.at[0], gzr.at[src], here).wait_recv()
    scale = F32(1.0 / (nq * left.shape[0]))
    grads = []
    for ref in (glr, zb):
        total = ref[0].astype(F32)
        for p in range(1, nq):
            total += ref[p].astype(F32)
        grads.append((total * scale).astype(BF16))
    adjoint(x_ref, gain_ref, w_ref, grads[0], grads[1], out_ref)

    for copy in sent:
        copy.wait_send()
    for o in range(nq):
        g2 = lax.rem(g + nq - o, nq)

        @pl.when(g2 != q)
        def _():
            send(right, rt.at[h, q], ps.at[o], pr.at[q], (g2, me)).wait_send()

        src = lax.rem(q + nq - o, nq)

        @pl.when(src != g)
        def _():
            send(pbuf.at[0], zb.at[g], gzs.at[o], gzr.at[g], (q, 2 * src + h)).wait_send()


def local(
    homolog_features,
    standardize_scale,
    left_factor_matrix,
    right_factor_matrix,
    final_mapping_matrix,
    final_offset_entries,
    incoming_sensitivity,
):
    seqs, residues, feats = homolog_features.shape
    chan = left_factor_matrix.shape[1]
    zdim = final_mapping_matrix.shape[1]
    cols = incoming_sensitivity.shape[1]
    nq = lax.axis_size("seq")
    wide = residues * chan

    def sds(*shape):
        return jax.ShapeDtypeStruct(shape, BF16)

    block = VMEM((nq, seqs, wide), BF16)
    x = homolog_features.reshape(seqs, residues * feats)
    w4 = jnp.concatenate([left_factor_matrix] * 4 + [right_factor_matrix] * 4, axis=1)
    pair, out = pl.pallas_call(
        functools.partial(kernel, nq, chan),
        out_shape=[sds(residues * cols, zdim), sds(seqs, residues * feats)],
        in_specs=[pl.BlockSpec(memory_space=VMEM)] * 6,
        out_specs=[pl.BlockSpec(memory_space=VMEM)] * 2,
        scratch_shapes=[
            VMEM((seqs, wide), BF16),
            VMEM((seqs, wide), BF16),
            block,
            VMEM((2, nq, seqs, wide), BF16),
            block,
            VMEM((residues * cols, zdim), F32),
            VMEM((cols // 4 * wide, 4 * chan), F32),
            VMEM((2, wide, cols * chan // 2), BF16),
        ]
        + [block] * 7
        + [pltpu.SemaphoreType.DMA((nq,))] * 16,
        compiler_params=pltpu.CompilerParams(
            vmem_limit_bytes=LIMIT, collective_id=0, has_side_effects=True
        ),
        name="outer_mean",
    )(
        x,
        standardize_scale.reshape(1, feats),
        w4,
        final_mapping_matrix,
        final_offset_entries.reshape(1, zdim),
        incoming_sensitivity.reshape(residues * cols, zdim),
    )
    return pair.reshape(residues, cols, zdim), out.reshape(seqs, residues, feats)


def solution(mesh):
    placed = (P("seq", "res", None), P(), P(), P(), P(), P(), P("res", "seq", None))
    return jax.shard_map(
        local,
        mesh=mesh,
        in_specs=placed,
        out_specs=(P("res", "seq", None), P("seq", "res", None)),
        check_vma=False,
    )
```

```python
import functools

import jax
import jax.numpy as jnp
from jax import lax
from jax.experimental import pallas as pl
from jax.experimental.pallas import tpu as pltpu
from jax.sharding import PartitionSpec as P

MESH = pl.DeviceIdType.MESH
F32, BF16 = jnp.float32, jnp.bfloat16
NT = (((1,), (1,)), ((), ()))
TN = (((0,), (0,)), ((), ()))
VMEM = pltpu.VMEM
LIMIT = 48 * 1024 * 1024


def place(nq):
    q = lax.axis_index("seq")
    r = lax.axis_index("res")
    return q, r // 2, lax.rem(r, 2)


def greet(nq, q, g, h):
    barrier = pltpu.get_barrier_semaphore()
    peers = [(q, 2 * g + 1 - h)]
    for o in range(1, nq):
        peers.append((lax.rem(q + o, nq), 2 * g + h))
        peers.append((q, 2 * lax.rem(g + o, nq) + h))
    for peer in peers:
        pl.semaphore_signal(barrier, inc=1, device_id=peer, device_id_type=MESH)
    return barrier, len(peers)


def send(src, dst, send_sem, recv_sem, device):
    return pltpu.make_async_remote_copy(
        src_ref=src, dst_ref=dst, send_sem=send_sem, recv_sem=recv_sem,
        device_id=device, device_id_type=MESH,
    )


def lanes_of(shape):
    return lax.broadcasted_iota(jnp.int32, shape, 1)


def spread(left_w_ref, right_w_ref, parts):
    feats, chan = left_w_ref.shape
    width = parts.shape[2]
    row = lax.broadcasted_iota(jnp.int32, (chan, width), 0)
    lane = lanes_of((chan, width))
    for m in range(4):
        total = jnp.zeros((feats, width), F32)
        for n, ref in enumerate((left_w_ref, right_w_ref)):
            pick = jnp.where(lane == row + (n * width // 2 + m * chan), F32(1), F32(0)).astype(BF16)
            total += jnp.dot(ref[...], pick, preferred_element_type=F32)
        parts[m] = total.astype(BF16)


def order(rows, chan):
    wide = rows * chan
    at = lax.broadcasted_iota(jnp.int32, (wide, 1), 0)
    to = lax.rem(at, chan) * rows + lax.div(at, chan)
    return jnp.where(lanes_of((wide, wide)) == to, F32(1), F32(0)).astype(BF16)


def project(x_ref, gain_ref, parts, hats, rstds, left, right):
    feats, width = parts.shape[1:]
    half = width // 2
    gain = gain_ref[...]
    residues = x_ref.shape[1] // feats
    for quad in range(residues // 4):
        acc = jnp.zeros((x_ref.shape[0], width), F32)
        for m in range(4):
            i = quad * 4 + m
            x = x_ref[:, i * feats : (i + 1) * feats].astype(F32)
            centred = x - jnp.mean(x, axis=-1, keepdims=True)
            rstd = lax.rsqrt(jnp.mean(centred * centred, axis=-1, keepdims=True) + 1e-05)
            hat = centred * rstd
            hats[:, i * feats : (i + 1) * feats] = hat
            rstds[i] = rstd
            acc += jnp.dot((hat * gain).astype(BF16), parts[m], preferred_element_type=F32)
        left[:, quad * half : (quad + 1) * half] = acc[:, :half].astype(BF16)
        right[:, quad * half : (quad + 1) * half] = acc[:, half:].astype(BF16)


def weight_block(map_ref, k, chan):
    rows = []
    for a in range(2):
        w = map_ref[pl.ds(pl.multiple_of((2 * k + a) * chan, chan), chan), :]
        zero = jnp.zeros_like(w)
        for m in range(4):
            rows.append(jnp.concatenate([w if n == m else zero for n in range(4)], axis=1))
    return jnp.concatenate(rows, axis=0)


def arrange(cot_ref, flat, out, quads):
    zdim = cot_ref.shape[1]
    cols = 4 * quads
    rows = cot_ref.shape[0] // cols
    flat[...] = cot_ref[...].astype(F32)
    for b in range(quads):
        for m in range(4):
            out[b * rows : (b + 1) * rows, m * zdim : (m + 1) * zdim] = flat[
                pl.ds(4 * b + m, rows, stride=cols), :
            ].astype(BF16)


def cotangent(chan, cots, map_ref, d, first, last):
    count = last - first
    high, wide = cots.shape[1:]
    lanes = 4 * chan
    quads = 2 * d.shape[3] // lanes
    rows = high // quads
    cot = cots[first:last].reshape(count * high, wide)

    def step(k, _):
        out = lax.dot_general(cot, weight_block(map_ref, k, chan), NT, preferred_element_type=F32)
        out = out.astype(BF16)
        for t in range(count):
            for a in range(2):
                for b in range(quads):
                    at = b % (quads // 2) * lanes
                    top = t * high + b * rows
                    d[
                        first + t, b // (quads // 2),
                        pl.ds(pl.multiple_of((2 * k + a) * rows, rows), rows), at : at + lanes,
                    ] = out[top : top + rows, a * lanes : (a + 1) * lanes]
        return 0

    lax.fori_loop(0, chan // 2, step, 0)


def pair_update(nq, chan, la, rt, map_ref, bias_ref, out_ref, flat, big):
    seqs, half = la.shape[1], rt.shape[3]
    lanes = 4 * chan
    quads = 2 * half // lanes
    rows = big.shape[1] // chan
    left = la[...].reshape(nq * seqs, la.shape[2])
    for a in range(2):
        right = rt[a].reshape(nq * seqs, half)
        big[a] = lax.dot_general(left, right, TN, preferred_element_type=F32).astype(BF16)

    def step(k, acc):
        def piece(a, b):
            at = b % (quads // 2) * lanes
            return big[
                b // (quads // 2), pl.ds(pl.multiple_of((2 * k + a) * rows, rows), rows), at : at + lanes
            ]

        lhs = jnp.concatenate(
            [jnp.concatenate([piece(a, b) for b in range(quads)], axis=0) for a in range(2)], axis=1
        )
        return acc + jnp.dot(lhs, weight_block(map_ref, k, chan), preferred_element_type=F32)

    zdim = map_ref.shape[1]
    acc = lax.fori_loop(0, chan // 2, step, jnp.zeros((quads * rows, 4 * zdim), F32))
    scale = F32(1.0 / (nq * seqs))
    for b in range(quads):
        for m in range(4):
            flat[pl.ds(4 * b + m, rows, stride=4 * quads), :] = (
                acc[b * rows : (b + 1) * rows, m * zdim : (m + 1) * zdim] * scale + bias_ref[...]
            )
    out_ref[...] = flat[...].astype(BF16)


def adjoint(gain_ref, parts, hats, rstds, gl, gr, out_ref):
    feats, width = parts.shape[1:]
    half = width // 2
    gain = gain_ref[...]
    residues = out_ref.shape[1] // feats
    for quad in range(residues // 4):
        cols = slice(quad * half, (quad + 1) * half)
        grads = jnp.concatenate([gl[:, cols], gr[:, cols]], axis=1)
        for m in range(4):
            i = quad * 4 + m
            hat = hats[:, i * feats : (i + 1) * feats]
            dy = lax.dot_general(grads, parts[m], NT, preferred_element_type=F32) * gain
            mean = jnp.mean(dy, axis=-1, keepdims=True)
            proj = jnp.mean(dy * hat, axis=-1, keepdims=True)
            out_ref[:, i * feats : (i + 1) * feats] = (rstds[i] * (dy - mean - hat * proj)).astype(BF16)


def kernel(
    nq, chan, x_ref, gain_ref, lw_ref, rw_ref, map_ref, bias_ref, cot_ref, pair_ref, out_ref,
    parts, hats, rstds, raw, left, right, la, rt, allr, cots, flat, big, d, grp, cbuf, sums, zb,
    ls, lr, zs, zr, as_, ar, ps, pr, cs, cr, rs, rr, gcs, gcr, gzs, gzr,
):
    q, g, h = place(nq)
    me = 2 * g + h
    here = (q, me)
    other = (q, 2 * g + 1 - h)
    seqs = left.shape[0]
    rows = left.shape[1] // chan
    barrier, peers = greet(nq, q, g, h)
    arrange(cot_ref, flat, cots.at[0], d.shape[3] * 2 // (4 * chan))
    spread(lw_ref, rw_ref, parts)
    project(x_ref, gain_ref, parts, hats, rstds, raw, right)
    perm = order(rows, chan)
    left[...] = jnp.dot(raw[...], perm, preferred_element_type=F32).astype(BF16)
    pl.semaphore_wait(barrier, peers)
    sent = []

    def start(*args):
        copy = send(*args)
        copy.start()
        sent.append(copy)

    for o in range(1, nq):
        start(right, allr.at[h, g], zs.at[o], zr.at[o], (q, 2 * lax.rem(g + o, nq) + h))
    for o in range(1, nq):
        start(cots.at[0], cots.at[o], as_.at[o], ar.at[o], (lax.rem(q + o, nq), me))
    for o in range(1, nq):
        start(left, la.at[q], ls.at[o], lr.at[o], (lax.rem(q + o, nq), me))
    la[q] = left[...]
    allr[h, g] = right[...]

    def grad_half(o):
        grp[o] = jnp.dot(left[...], d[o, 1 - h], preferred_element_type=F32).astype(BF16)
        start(grp.at[o], cbuf.at[o], gcs.at[o], gcr.at[o], other)

    def grad_sum(o):
        total = jnp.dot(left[...], d[o, h], preferred_element_type=F32)
        send(grp.at[o], cbuf.at[o], gcs.at[o], gcr.at[o], here).wait_recv()
        sums[o] = (total + cbuf[o].astype(F32)).astype(BF16)
        tile = lax.rem(q + nq - o, nq)

        @pl.when(tile != g)
        def _():
            send(sums.at[o], zb.at[g], gzs.at[o], gzr.at[g], (q, 2 * tile + h)).start()

        @pl.when(tile == g)
        def _():
            zb[g] = sums[o]

    cotangent(chan, cots, map_ref, d, 0, 1)
    grad_half(0)
    grad_sum(0)
    for o in range(1, nq):
        send(cots.at[0], cots.at[o], as_.at[o], ar.at[o], here).wait_recv()
    cotangent(chan, cots, map_ref, d, 1, nq)
    for o in range(1, nq):
        grad_half(o)
    for o in range(1, nq):
        grad_sum(o)

    def forward_right(o, g2):
        src = allr.at[h, g2]
        start(src, src, rs.at[o], rr.at[o], other)

        @pl.when(g2 != q)
        def _():
            send(src, rt.at[h, q], ps.at[o], pr.at[q], (g2, me)).start()

        @pl.when(g2 == q)
        def _():
            rt[h, q] = src[...]

    for o in range(nq):
        g2 = lax.rem(g + nq - o, nq)
        if o:
            send(right, allr.at[h, g2], zs.at[o], zr.at[o], here).wait_recv()
        forward_right(o, g2)

    for o in range(nq):
        g2 = lax.rem(g + nq - o, nq)
        send(allr.at[h, g2], allr.at[1 - h, g2], rs.at[o], rr.at[o], here).wait_recv()
    total = jnp.zeros(left.shape, F32)
    for o in range(nq):
        tile = lax.rem(q + nq - o, nq)
        for a in range(2):
            total += lax.dot_general(allr[a, tile], d[o, a], NT, preferred_element_type=F32)
    scale = F32(1.0 / (nq * seqs))
    gl = (total * scale).astype(BF16)
    gl = lax.dot_general(gl, perm, NT, preferred_element_type=F32).astype(BF16)

    for p in range(nq):
        src = lax.rem(q + nq - p, nq)
        if p:
            send(right, rt.at[h, src], ps.at[0], pr.at[src], here).wait_recv()
        start(rt.at[h, src], rt.at[h, src], cs.at[p], cr.at[p], other)
    for o in range(1, nq):
        src = lax.rem(q + nq - o, nq)
        send(left, la.at[src], ls.at[o], lr.at[o], here).wait_recv()
    for p in range(nq):
        src = lax.rem(q + nq - p, nq)
        send(rt.at[h, src], rt.at[1 - h, src], cs.at[p], cr.at[p], here).wait_recv()
    pair_update(nq, chan, la, rt, map_ref, bias_ref, pair_ref, flat, big)

    for p in range(1, nq):
        src = lax.rem(g + p, nq)
        send(sums.at[0], zb.at[src], gzs.at[0], gzr.at[src], here).wait_recv()
    total = zb[0].astype(F32)
    for p in range(1, nq):
        total += zb[p].astype(F32)
    adjoint(gain_ref, parts, hats, rstds, gl, (total * scale).astype(BF16), out_ref)

    for copy in sent:
        copy.wait_send()
    for o in range(nq):
        g2 = lax.rem(g + nq - o, nq)

        @pl.when(g2 != q)
        def _():
            send(allr.at[h, g2], rt.at[h, q], ps.at[o], pr.at[q], (g2, me)).wait_send()

        tile = lax.rem(q + nq - o, nq)

        @pl.when(tile != g)
        def _():
            send(sums.at[o], zb.at[g], gzs.at[o], gzr.at[g], (q, 2 * tile + h)).wait_send()


def local(
    homolog_features,
    standardize_scale,
    left_factor_matrix,
    right_factor_matrix,
    final_mapping_matrix,
    final_offset_entries,
    incoming_sensitivity,
):
    seqs, residues, feats = homolog_features.shape
    chan = left_factor_matrix.shape[1]
    zdim = final_mapping_matrix.shape[1]
    cols = incoming_sensitivity.shape[1]
    nq = lax.axis_size("seq")
    wide = residues * chan

    def sds(*shape):
        return jax.ShapeDtypeStruct(shape, BF16)

    one = VMEM((seqs, wide), BF16)
    block = VMEM((nq, seqs, wide), BF16)
    both = VMEM((2, nq, seqs, wide), BF16)
    half = cols * chan // 2
    pair, out = pl.pallas_call(
        functools.partial(kernel, nq, chan),
        out_shape=[sds(residues * cols, zdim), sds(seqs, residues * feats)],
        in_specs=[pl.BlockSpec(memory_space=VMEM)] * 7,
        out_specs=[pl.BlockSpec(memory_space=VMEM)] * 2,
        scratch_shapes=[
            VMEM((4, feats, 8 * chan), BF16),
            VMEM((seqs, residues * feats), F32),
            VMEM((residues, seqs, 1), F32),
            one,
            one,
            one,
            block,
            both,
            both,
            VMEM((nq, cols // 4 * residues, 4 * zdim), BF16),
            VMEM((residues * cols, zdim), F32),
            VMEM((2, wide, half), BF16),
            VMEM((nq, 2, wide, half), BF16),
        ]
        + [block] * 4
        + [pltpu.SemaphoreType.DMA((nq,))] * 16,
        compiler_params=pltpu.CompilerParams(
            vmem_limit_bytes=LIMIT, collective_id=0, has_side_effects=True
        ),
        name="outer_mean",
    )(
        homolog_features.reshape(seqs, residues * feats),
        standardize_scale.reshape(1, feats),
        left_factor_matrix,
        right_factor_matrix,
        final_mapping_matrix,
        final_offset_entries.reshape(1, zdim),
        incoming_sensitivity.reshape(residues * cols, zdim),
    )
    return pair.reshape(residues, cols, zdim), out.reshape(seqs, residues, feats)


def solution(mesh):
    placed = (P("seq", "res", None), P(), P(), P(), P(), P(), P("res", "seq", None))
    return jax.shard_map(
        local,
        mesh=mesh,
        in_specs=placed,
        out_specs=(P("res", "seq", None), P("seq", "res", None)),
        check_vma=False,
    )
```

```python
import functools

import jax
import jax.numpy as jnp
from jax import lax
from jax.experimental import pallas as pl
from jax.experimental.pallas import tpu as pltpu
from jax.sharding import PartitionSpec as P

MESH = pl.DeviceIdType.MESH
F32, BF16 = jnp.float32, jnp.bfloat16
NT = (((1,), (1,)), ((), ()))
TN = (((0,), (0,)), ((), ()))
VMEM = pltpu.VMEM
LIMIT = 64000 * 1024


def place(nq):
    q = lax.axis_index("seq")
    r = lax.axis_index("res")
    return q, r // 2, lax.rem(r, 2)


def greet(nq, q, g, h):
    barrier = pltpu.get_barrier_semaphore()
    peers = [(q, 2 * g + 1 - h)]
    for o in range(1, nq):
        peers.append((lax.rem(q + o, nq), 2 * g + h))
        peers.append((q, 2 * lax.rem(g + o, nq) + h))
    for peer in peers:
        pl.semaphore_signal(barrier, inc=1, device_id=peer, device_id_type=MESH)
    return barrier, len(peers)


def send(src, dst, send_sem, recv_sem, device):
    return pltpu.make_async_remote_copy(
        src_ref=src, dst_ref=dst, send_sem=send_sem, recv_sem=recv_sem,
        device_id=device, device_id_type=MESH,
    )


def lanes_of(shape):
    return lax.broadcasted_iota(jnp.int32, shape, 1)


def spread(left_w_ref, right_w_ref, parts):
    chan, feats = left_w_ref.shape
    width = parts.shape[2]
    row = lax.broadcasted_iota(jnp.int32, (chan, width), 0)
    lane = lanes_of((chan, width))
    for m in range(4):
        total = jnp.zeros((feats, width), F32)
        for n, ref in enumerate((left_w_ref, right_w_ref)):
            pick = jnp.where(lane == row + (n * width // 2 + m * chan), F32(1), F32(0)).astype(BF16)
            total += lax.dot_general(ref[...], pick, TN, preferred_element_type=F32)
        parts[m] = total.astype(BF16)


def order(rows, chan):
    wide = rows * chan
    at = lax.broadcasted_iota(jnp.int32, (wide, 1), 0)
    to = lax.rem(at, chan) * rows + lax.div(at, chan)
    return jnp.where(lanes_of((wide, wide)) == to, F32(1), F32(0)).astype(BF16)


def project(x_ref, gain_ref, parts, xs, hats, rstds, left, right):
    feats, width = parts.shape[1:]
    half = width // 2
    gain = gain_ref[...]
    residues = rstds.shape[0]
    seqs = left.shape[0]
    total = x_ref.shape[0]
    for n in range(feats // 128):
        xs[n * total : (n + 1) * total, :] = x_ref[:, n * 128 : (n + 1) * 128].astype(F32)
    for quad in range(residues // 4):
        acc = jnp.zeros((seqs, width), F32)
        for m in range(4):
            i = quad * 4 + m
            x = jnp.concatenate(
                [xs[pl.ds(n * total + i, seqs, stride=residues), :] for n in range(feats // 128)], axis=1
            )
            centred = x - jnp.mean(x, axis=-1, keepdims=True)
            rstd = lax.rsqrt(jnp.mean(centred * centred, axis=-1, keepdims=True) + 1e-05)
            hat = centred * rstd
            hats[:, i * feats : (i + 1) * feats] = hat
            rstds[i] = rstd
            acc += jnp.dot((hat * gain).astype(BF16), parts[m], preferred_element_type=F32)
        left[:, quad * half : (quad + 1) * half] = acc[:, :half].astype(BF16)
        right[:, quad * half : (quad + 1) * half] = acc[:, half:].astype(BF16)


def weight_block(map_ref, k, chan):
    rows = []
    for a in range(2):
        w = map_ref[pl.ds(pl.multiple_of((2 * k + a) * chan, chan), chan), :]
        zero = jnp.zeros_like(w)
        for m in range(4):
            rows.append(jnp.concatenate([w if n == m else zero for n in range(4)], axis=1))
    return jnp.concatenate(rows, axis=0)


def arrange(cot_ref, flat, out, quads):
    zdim = cot_ref.shape[1]
    cols = 4 * quads
    rows = cot_ref.shape[0] // cols
    flat[...] = cot_ref[...].astype(F32)
    for b in range(quads):
        for m in range(4):
            out[b * rows : (b + 1) * rows, m * zdim : (m + 1) * zdim] = flat[
                pl.ds(4 * b + m, rows, stride=cols), :
            ].astype(BF16)


def cotangent(chan, cots, map_ref, d, first, last):
    count = last - first
    high, wide = cots.shape[1:]
    lanes = 4 * chan
    quads = 2 * d.shape[3] // lanes
    rows = high // quads
    cot = cots[first:last].reshape(count * high, wide)

    def step(k, _):
        out = lax.dot_general(cot, weight_block(map_ref, k, chan), NT, preferred_element_type=F32)
        out = out.astype(BF16)
        for t in range(count):
            for a in range(2):
                for b in range(quads):
                    at = b % (quads // 2) * lanes
                    top = t * high + b * rows
                    d[
                        first + t, b // (quads // 2),
                        pl.ds(pl.multiple_of((2 * k + a) * rows, rows), rows), at : at + lanes,
                    ] = out[top : top + rows, a * lanes : (a + 1) * lanes]
        return 0

    lax.fori_loop(0, chan // 2, step, 0)


def pair_update(nq, chan, la, rt, map_ref, bias_ref, out_ref, flat, big):
    seqs, half = la.shape[1], rt.shape[3]
    lanes = 4 * chan
    quads = 2 * half // lanes
    rows = big.shape[1] // chan
    left = la[...].reshape(nq * seqs, la.shape[2])
    for a in range(2):
        right = rt[a].reshape(nq * seqs, half)
        big[a] = lax.dot_general(left, right, TN, preferred_element_type=F32).astype(BF16)

    def step(k, acc):
        def piece(a, b):
            at = b % (quads // 2) * lanes
            return big[
                b // (quads // 2), pl.ds(pl.multiple_of((2 * k + a) * rows, rows), rows), at : at + lanes
            ]

        lhs = jnp.concatenate(
            [jnp.concatenate([piece(a, b) for b in range(quads)], axis=0) for a in range(2)], axis=1
        )
        return acc + jnp.dot(lhs, weight_block(map_ref, k, chan), preferred_element_type=F32)

    zdim = map_ref.shape[1]
    acc = lax.fori_loop(0, chan // 2, step, jnp.zeros((quads * rows, 4 * zdim), F32))
    scale = F32(1.0 / (nq * seqs))
    for b in range(quads):
        for m in range(4):
            flat[pl.ds(4 * b + m, rows, stride=4 * quads), :] = (
                acc[b * rows : (b + 1) * rows, m * zdim : (m + 1) * zdim] * scale + bias_ref[...]
            )
    out_ref[...] = flat[...].astype(BF16)


def adjoint(gain_ref, parts, hats, rstds, gl, gr, out_ref):
    feats, width = parts.shape[1:]
    half = width // 2
    gain = gain_ref[...]
    residues = out_ref.shape[1] // feats
    for quad in range(residues // 4):
        cols = slice(quad * half, (quad + 1) * half)
        grads = jnp.concatenate([gl[:, cols], gr[:, cols]], axis=1)
        for m in range(4):
            i = quad * 4 + m
            hat = hats[:, i * feats : (i + 1) * feats]
            dy = lax.dot_general(grads, parts[m], NT, preferred_element_type=F32) * gain
            mean = jnp.mean(dy, axis=-1, keepdims=True)
            proj = jnp.mean(dy * hat, axis=-1, keepdims=True)
            out_ref[:, i * feats : (i + 1) * feats] = (rstds[i] * (dy - mean - hat * proj)).astype(BF16)


def kernel(
    nq, chan, x_in, gain_in, lw_in, rw_in, map_in, bias_in, cot_in, pair_ref, out_ref,
    x_ref, gain_ref, lw_ref, rw_ref, map_ref, bias_ref, cot_ref,
    parts, xs, hats, rstds, raw, left, right, la, rt, allr, cots, flat, big, d, grp, cbuf, sums, zb,
    ls, lr, zs, zr, as_, ar, ps, pr, cs, cr, rs, rr, gcs, gcr, gzs, gzr, ins,
):
    q, g, h = place(nq)
    me = 2 * g + h
    here = (q, me)
    other = (q, 2 * g + 1 - h)
    seqs = left.shape[0]
    rows = left.shape[1] // chan
    loads = [
        pltpu.make_async_copy(src, dst, ins.at[n])
        for n, (src, dst) in enumerate(
            [(cot_in, cot_ref), (x_in, x_ref), (lw_in, lw_ref), (rw_in, rw_ref), (gain_in, gain_ref),
             (map_in, map_ref), (bias_in, bias_ref)]
        )
    ]
    for load in loads:
        load.start()
    barrier, peers = greet(nq, q, g, h)
    loads[0].wait()
    arrange(cot_ref, flat, cots.at[0], d.shape[3] * 2 // (4 * chan))
    loads[2].wait()
    loads[3].wait()
    spread(lw_ref, rw_ref, parts)
    pl.semaphore_wait(barrier, peers)
    sent = []

    def start(*args):
        copy = send(*args)
        copy.start()
        sent.append(copy)

    for o in range(1, nq):
        start(cots.at[0], cots.at[o], as_.at[o], ar.at[o], (lax.rem(q + o, nq), me))
    loads[1].wait()
    loads[4].wait()
    project(x_ref, gain_ref, parts, xs, hats, rstds, raw, right)
    for o in range(1, nq):
        start(right, allr.at[h, g], zs.at[o], zr.at[o], (q, 2 * lax.rem(g + o, nq) + h))
    perm = order(rows, chan)
    left[...] = jnp.dot(raw[...], perm, preferred_element_type=F32).astype(BF16)
    for o in range(1, nq):
        start(left, la.at[q], ls.at[o], lr.at[o], (lax.rem(q + o, nq), me))
    la[q] = left[...]
    allr[h, g] = right[...]

    def grad_half(o):
        grp[o] = jnp.dot(left[...], d[o, 1 - h], preferred_element_type=F32).astype(BF16)
        start(grp.at[o], cbuf.at[o], gcs.at[o], gcr.at[o], other)

    def grad_sum(o):
        total = jnp.dot(left[...], d[o, h], preferred_element_type=F32)
        send(grp.at[o], cbuf.at[o], gcs.at[o], gcr.at[o], here).wait_recv()
        sums[o] = (total + cbuf[o].astype(F32)).astype(BF16)
        tile = lax.rem(q + nq - o, nq)

        @pl.when(tile != g)
        def _():
            send(sums.at[o], zb.at[g], gzs.at[o], gzr.at[g], (q, 2 * tile + h)).start()

        @pl.when(tile == g)
        def _():
            zb[g] = sums[o]

    loads[5].wait()
    loads[6].wait()
    cotangent(chan, cots, map_ref, d, 0, 1)
    grad_half(0)
    for o in range(1, nq):
        send(cots.at[0], cots.at[o], as_.at[o], ar.at[o], here).wait_recv()
    cotangent(chan, cots, map_ref, d, 1, nq)
    for o in range(1, nq):
        grad_half(o)

    def forward_right(o, g2):
        src = allr.at[h, g2]
        start(src, src, rs.at[o], rr.at[o], other)

        @pl.when(g2 != q)
        def _():
            send(src, rt.at[h, q], ps.at[o], pr.at[q], (g2, me)).start()

        @pl.when(g2 == q)
        def _():
            rt[h, q] = src[...]

    for o in range(nq):
        g2 = lax.rem(g + nq - o, nq)
        if o:
            send(right, allr.at[h, g2], zs.at[o], zr.at[o], here).wait_recv()
        forward_right(o, g2)
    for o in range(nq):
        grad_sum(o)

    for o in range(nq):
        g2 = lax.rem(g + nq - o, nq)
        send(allr.at[h, g2], allr.at[1 - h, g2], rs.at[o], rr.at[o], here).wait_recv()
    total = jnp.zeros(left.shape, F32)
    for o in range(nq):
        tile = lax.rem(q + nq - o, nq)
        for a in range(2):
            total += lax.dot_general(allr[a, tile], d[o, a], NT, preferred_element_type=F32)
    scale = F32(1.0 / (nq * seqs))
    gl = (total * scale).astype(BF16)
    gl = lax.dot_general(gl, perm, NT, preferred_element_type=F32).astype(BF16)

    for p in range(nq):
        src = lax.rem(q + nq - p, nq)
        if p:
            send(right, rt.at[h, src], ps.at[0], pr.at[src], here).wait_recv()
        start(rt.at[h, src], rt.at[h, src], cs.at[p], cr.at[p], other)
    for o in range(1, nq):
        src = lax.rem(q + nq - o, nq)
        send(left, la.at[src], ls.at[o], lr.at[o], here).wait_recv()
    for p in range(nq):
        src = lax.rem(q + nq - p, nq)
        send(rt.at[h, src], rt.at[1 - h, src], cs.at[p], cr.at[p], here).wait_recv()
    pair_update(nq, chan, la, rt, map_ref, bias_ref, pair_ref, flat, big)

    for p in range(1, nq):
        src = lax.rem(g + p, nq)
        send(sums.at[0], zb.at[src], gzs.at[0], gzr.at[src], here).wait_recv()
    total = zb[0].astype(F32)
    for p in range(1, nq):
        total += zb[p].astype(F32)
    adjoint(gain_ref, parts, hats, rstds, gl, (total * scale).astype(BF16), out_ref)

    for copy in sent:
        copy.wait_send()
    for o in range(nq):
        g2 = lax.rem(g + nq - o, nq)

        @pl.when(g2 != q)
        def _():
            send(allr.at[h, g2], rt.at[h, q], ps.at[o], pr.at[q], (g2, me)).wait_send()

        tile = lax.rem(q + nq - o, nq)

        @pl.when(tile != g)
        def _():
            send(sums.at[o], zb.at[g], gzs.at[o], gzr.at[g], (q, 2 * tile + h)).wait_send()


def local(
    homolog_features,
    standardize_scale,
    left_factor_matrix,
    right_factor_matrix,
    final_mapping_matrix,
    final_offset_entries,
    incoming_sensitivity,
):
    seqs, residues, feats = homolog_features.shape
    chan = left_factor_matrix.shape[1]
    zdim = final_mapping_matrix.shape[1]
    cols = incoming_sensitivity.shape[1]
    nq = lax.axis_size("seq")
    wide = residues * chan

    def sds(*shape):
        return jax.ShapeDtypeStruct(shape, BF16)

    one = VMEM((seqs, wide), BF16)
    block = VMEM((nq, seqs, wide), BF16)
    both = VMEM((2, nq, seqs, wide), BF16)
    half = cols * chan // 2
    pair, out = pl.pallas_call(
        functools.partial(kernel, nq, chan),
        out_shape=[sds(residues * cols, zdim), sds(seqs, residues * feats)],
        in_specs=[pl.BlockSpec(memory_space=pltpu.HBM)] * 7,
        out_specs=[pl.BlockSpec(memory_space=VMEM)] * 2,
        scratch_shapes=[
            VMEM((seqs * residues, feats), BF16),
            VMEM((1, feats), F32),
            VMEM((chan, feats), BF16),
            VMEM((chan, feats), BF16),
            VMEM((chan * chan, zdim), BF16),
            VMEM((1, zdim), F32),
            VMEM((residues * cols, zdim), BF16),
            VMEM((4, feats, 8 * chan), BF16),
            VMEM((feats // 128 * seqs * residues, 128), F32),
            VMEM((seqs, residues * feats), F32),
            VMEM((residues, seqs, 1), F32),
            one,
            one,
            one,
            block,
            both,
            both,
            VMEM((nq, cols // 4 * residues, 4 * zdim), BF16),
            VMEM((residues * cols, zdim), F32),
            VMEM((2, wide, half), BF16),
            VMEM((nq, 2, wide, half), BF16),
        ]
        + [block] * 4
        + [pltpu.SemaphoreType.DMA((nq,))] * 16
        + [pltpu.SemaphoreType.DMA((7,))],
        compiler_params=pltpu.CompilerParams(
            vmem_limit_bytes=LIMIT, collective_id=0, has_side_effects=True
        ),
        name="outer_mean",
    )(
        homolog_features.reshape(seqs * residues, feats),
        standardize_scale.reshape(1, feats),
        jnp.transpose(left_factor_matrix),
        jnp.transpose(right_factor_matrix),
        final_mapping_matrix,
        final_offset_entries.reshape(1, zdim),
        incoming_sensitivity.reshape(residues * cols, zdim),
    )
    return pair.reshape(residues, cols, zdim), out.reshape(seqs, residues, feats)


def solution(mesh):
    placed = (P("seq", "res", None), P(), P(), P(), P(), P(), P("res", "seq", None))
    return jax.shard_map(
        local,
        mesh=mesh,
        in_specs=placed,
        out_specs=(P("res", "seq", None), P("seq", "res", None)),
        check_vma=False,
    )
```

```python
import functools

import jax
import jax.numpy as jnp
from jax import lax
from jax.experimental import pallas as pl
from jax.experimental.pallas import tpu as pltpu
from jax.sharding import PartitionSpec as P

MESH = pl.DeviceIdType.MESH
F32, BF16 = jnp.float32, jnp.bfloat16
NT = (((1,), (1,)), ((), ()))
TN = (((0,), (0,)), ((), ()))
VMEM = pltpu.VMEM
LIMIT = 64000 * 1024


def place(nq):
    q = lax.axis_index("seq")
    r = lax.axis_index("res")
    return q, r // 2, lax.rem(r, 2)


def greet(nq, q, g, h):
    barrier = pltpu.get_barrier_semaphore()
    peers = [(q, 2 * g + 1 - h)]
    for o in range(1, nq):
        peers.append((lax.rem(q + o, nq), 2 * g + h))
        peers.append((q, 2 * lax.rem(g + o, nq) + h))
    for peer in peers:
        pl.semaphore_signal(barrier, inc=1, device_id=peer, device_id_type=MESH)
    return barrier, len(peers)


def send(src, dst, send_sem, recv_sem, device):
    return pltpu.make_async_remote_copy(
        src_ref=src, dst_ref=dst, send_sem=send_sem, recv_sem=recv_sem,
        device_id=device, device_id_type=MESH,
    )


def lanes_of(shape):
    return lax.broadcasted_iota(jnp.int32, shape, 1)


def spread(left_w_ref, right_w_ref, parts):
    chan, feats = left_w_ref.shape
    width = parts.shape[2]
    row = lax.broadcasted_iota(jnp.int32, (chan, width), 0)
    lane = lanes_of((chan, width))
    for m in range(4):
        total = jnp.zeros((feats, width), F32)
        for n, ref in enumerate((left_w_ref, right_w_ref)):
            pick = jnp.where(lane == row + (n * width // 2 + m * chan), F32(1), F32(0)).astype(BF16)
            total += lax.dot_general(ref[...], pick, TN, preferred_element_type=F32)
        parts[m] = total.astype(BF16)


def order(rows, chan):
    wide = rows * chan
    at = lax.broadcasted_iota(jnp.int32, (wide, 1), 0)
    to = lax.rem(at, chan) * rows + lax.div(at, chan)
    return jnp.where(lanes_of((wide, wide)) == to, F32(1), F32(0)).astype(BF16)


def project(x_ref, gain_ref, parts, xs, hats, rstds, left, right):
    feats, width = parts.shape[1:]
    half = width // 2
    gain = gain_ref[...]
    residues = rstds.shape[0]
    seqs = left.shape[0]
    total = x_ref.shape[0]
    for n in range(feats // 128):
        xs[n * total : (n + 1) * total, :] = x_ref[:, n * 128 : (n + 1) * 128].astype(F32)
    for quad in range(residues // 4):
        acc = jnp.zeros((seqs, width), F32)
        for m in range(4):
            i = quad * 4 + m
            x = jnp.concatenate(
                [xs[pl.ds(n * total + i, seqs, stride=residues), :] for n in range(feats // 128)], axis=1
            )
            centred = x - jnp.mean(x, axis=-1, keepdims=True)
            rstd = lax.rsqrt(jnp.mean(centred * centred, axis=-1, keepdims=True) + 1e-05)
            hat = centred * rstd
            hats[:, i * feats : (i + 1) * feats] = hat
            rstds[i] = rstd
            acc += jnp.dot((hat * gain).astype(BF16), parts[m], preferred_element_type=F32)
        left[:, quad * half : (quad + 1) * half] = acc[:, :half].astype(BF16)
        right[:, quad * half : (quad + 1) * half] = acc[:, half:].astype(BF16)


def weight_block(map_ref, k, chan):
    rows = []
    for a in range(2):
        w = map_ref[pl.ds(pl.multiple_of((2 * k + a) * chan, chan), chan), :]
        zero = jnp.zeros_like(w)
        for m in range(4):
            rows.append(jnp.concatenate([w if n == m else zero for n in range(4)], axis=1))
    return jnp.concatenate(rows, axis=0)


def arrange(cot_ref, flat, out, quads):
    zdim = cot_ref.shape[1]
    cols = 4 * quads
    rows = cot_ref.shape[0] // cols
    flat[...] = cot_ref[...].astype(F32)
    for b in range(quads):
        for m in range(4):
            out[b * rows : (b + 1) * rows, m * zdim : (m + 1) * zdim] = flat[
                pl.ds(4 * b + m, rows, stride=cols), :
            ].astype(BF16)


def cotangent(chan, cots, map_ref, d, first, last):
    count = last - first
    high, wide = cots.shape[1:]
    lanes = 4 * chan
    quads = 2 * d.shape[3] // lanes
    rows = high // quads
    cot = cots[first:last].reshape(count * high, wide)

    def step(k, _):
        out = lax.dot_general(cot, weight_block(map_ref, k, chan), NT, preferred_element_type=F32)
        out = out.astype(BF16)
        for t in range(count):
            for a in range(2):
                for b in range(quads):
                    at = b % (quads // 2) * lanes
                    top = t * high + b * rows
                    d[
                        first + t, b // (quads // 2),
                        pl.ds(pl.multiple_of((2 * k + a) * rows, rows), rows), at : at + lanes,
                    ] = out[top : top + rows, a * lanes : (a + 1) * lanes]
        return 0

    lax.fori_loop(0, chan // 2, step, 0)


def pair_update(nq, chan, la, rt, map_ref, bias_ref, out_ref, flat, big):
    seqs, half = la.shape[1], rt.shape[3]
    lanes = 4 * chan
    quads = 2 * half // lanes
    rows = big.shape[1] // chan
    left = la[...].reshape(nq * seqs, la.shape[2])
    for a in range(2):
        right = rt[a].reshape(nq * seqs, half)
        big[a] = lax.dot_general(left, right, TN, preferred_element_type=F32).astype(BF16)

    def step(k, acc):
        def piece(a, b):
            at = b % (quads // 2) * lanes
            return big[
                b // (quads // 2), pl.ds(pl.multiple_of((2 * k + a) * rows, rows), rows), at : at + lanes
            ]

        lhs = jnp.concatenate(
            [jnp.concatenate([piece(a, b) for b in range(quads)], axis=0) for a in range(2)], axis=1
        )
        return acc + jnp.dot(lhs, weight_block(map_ref, k, chan), preferred_element_type=F32)

    zdim = map_ref.shape[1]
    acc = lax.fori_loop(0, chan // 2, step, jnp.zeros((quads * rows, 4 * zdim), F32))
    scale = F32(1.0 / (nq * seqs))
    for b in range(quads):
        for m in range(4):
            flat[pl.ds(4 * b + m, rows, stride=4 * quads), :] = (
                acc[b * rows : (b + 1) * rows, m * zdim : (m + 1) * zdim] * scale + bias_ref[...]
            )
    out_ref[...] = flat[...].astype(BF16)


def adjoint(gain_ref, parts, hats, rstds, gl, gr, out_ref):
    feats, width = parts.shape[1:]
    half = width // 2
    gain = gain_ref[...]
    residues = out_ref.shape[1] // feats
    for quad in range(residues // 4):
        cols = slice(quad * half, (quad + 1) * half)
        grads = jnp.concatenate([gl[:, cols], gr[:, cols]], axis=1)
        for m in range(4):
            i = quad * 4 + m
            hat = hats[:, i * feats : (i + 1) * feats]
            dy = lax.dot_general(grads, parts[m], NT, preferred_element_type=F32) * gain
            mean = jnp.mean(dy, axis=-1, keepdims=True)
            proj = jnp.mean(dy * hat, axis=-1, keepdims=True)
            out_ref[:, i * feats : (i + 1) * feats] = (rstds[i] * (dy - mean - hat * proj)).astype(BF16)


def kernel(
    nq, chan, x_in, gain_in, lw_in, rw_in, map_in, bias_in, cot_in, pair_ref, out_ref,
    tots, x_ref, gain_ref, lw_ref, rw_ref, map_ref, bias_ref, cot_ref,
    parts, xs, hats, rstds, raw, left, right, la, rt, allr, cots, flat, big, d, grp, cbuf, sums, zb,
    ls, lr, zs, zr, as_, ar, ps, pr, cs, cr, rs, rr, gcs, gcr, gzs, gzr, ins,
):
    q, g, h = place(nq)
    me = 2 * g + h
    here = (q, me)
    other = (q, 2 * g + 1 - h)
    seqs = left.shape[0]
    rows = left.shape[1] // chan
    loads = [
        pltpu.make_async_copy(src, dst, ins.at[n])
        for n, (src, dst) in enumerate(
            [(cot_in, cot_ref), (x_in, x_ref), (lw_in, lw_ref), (rw_in, rw_ref), (gain_in, gain_ref),
             (map_in, map_ref), (bias_in, bias_ref)]
        )
    ]
    for load in loads:
        load.start()
    barrier, peers = greet(nq, q, g, h)
    loads[0].wait()
    arrange(cot_ref, flat, cots.at[0], d.shape[3] * 2 // (4 * chan))
    loads[2].wait()
    loads[3].wait()
    spread(lw_ref, rw_ref, parts)
    pl.semaphore_wait(barrier, peers)
    sent = []

    def start(*args):
        copy = send(*args)
        copy.start()
        sent.append(copy)

    for o in range(1, nq):
        start(cots.at[0], cots.at[o], as_.at[o], ar.at[o], (lax.rem(q + o, nq), me))
    loads[1].wait()
    loads[4].wait()
    project(x_ref, gain_ref, parts, xs, hats, rstds, raw, right)
    for o in range(1, nq):
        start(right, allr.at[h, g], zs.at[o], zr.at[o], (q, 2 * lax.rem(g + o, nq) + h))
    perm = order(rows, chan)
    left[...] = jnp.dot(raw[...], perm, preferred_element_type=F32).astype(BF16)
    la[q] = left[...]
    allr[h, g] = right[...]

    def grad_half(o):
        grp[o] = jnp.dot(left[...], d[o, 1 - h], preferred_element_type=F32).astype(BF16)
        start(grp.at[o], cbuf.at[o], gcs.at[o], gcr.at[o], other)

    def grad_sum(o):
        send(grp.at[o], cbuf.at[o], gcs.at[o], gcr.at[o], here).wait_recv()
        sums[o] = (tots[o] + cbuf[o].astype(F32)).astype(BF16)
        tile = lax.rem(q + nq - o, nq)

        @pl.when(tile != g)
        def _():
            send(sums.at[o], zb.at[g], gzs.at[o], gzr.at[g], (q, 2 * tile + h)).start()

        @pl.when(tile == g)
        def _():
            zb[g] = sums[o]

    loads[5].wait()
    loads[6].wait()
    cotangent(chan, cots, map_ref, d, 0, 1)
    grad_half(0)
    for o in range(1, nq):
        start(left, la.at[q], ls.at[o], lr.at[o], (lax.rem(q + o, nq), me))
    for o in range(1, nq):
        send(cots.at[0], cots.at[o], as_.at[o], ar.at[o], here).wait_recv()
    cotangent(chan, cots, map_ref, d, 1, nq)
    for o in range(1, nq):
        grad_half(o)
    for o in range(nq):
        tots[o] = jnp.dot(left[...], d[o, h], preferred_element_type=F32)

    def forward_right(o, g2):
        src = allr.at[h, g2]
        start(src, src, rs.at[o], rr.at[o], other)

        @pl.when(g2 != q)
        def _():
            send(src, rt.at[h, q], ps.at[o], pr.at[q], (g2, me)).start()

        @pl.when(g2 == q)
        def _():
            rt[h, q] = src[...]

    for o in range(nq):
        g2 = lax.rem(g + nq - o, nq)
        if o:
            send(right, allr.at[h, g2], zs.at[o], zr.at[o], here).wait_recv()
        forward_right(o, g2)
    for o in range(nq):
        grad_sum(o)

    for o in range(nq):
        g2 = lax.rem(g + nq - o, nq)
        send(allr.at[h, g2], allr.at[1 - h, g2], rs.at[o], rr.at[o], here).wait_recv()
    total = jnp.zeros(left.shape, F32)
    for o in range(nq):
        tile = lax.rem(q + nq - o, nq)
        for a in range(2):
            total += lax.dot_general(allr[a, tile], d[o, a], NT, preferred_element_type=F32)
    scale = F32(1.0 / (nq * seqs))
    gl = (total * scale).astype(BF16)
    gl = lax.dot_general(gl, perm, NT, preferred_element_type=F32).astype(BF16)

    for p in range(nq):
        src = lax.rem(q + nq - p, nq)
        if p:
            send(right, rt.at[h, src], ps.at[0], pr.at[src], here).wait_recv()
        start(rt.at[h, src], rt.at[h, src], cs.at[p], cr.at[p], other)
    for o in range(1, nq):
        src = lax.rem(q + nq - o, nq)
        send(left, la.at[src], ls.at[o], lr.at[o], here).wait_recv()
    for p in range(nq):
        src = lax.rem(q + nq - p, nq)
        send(rt.at[h, src], rt.at[1 - h, src], cs.at[p], cr.at[p], here).wait_recv()
    pair_update(nq, chan, la, rt, map_ref, bias_ref, pair_ref, flat, big)

    for p in range(1, nq):
        src = lax.rem(g + p, nq)
        send(sums.at[0], zb.at[src], gzs.at[0], gzr.at[src], here).wait_recv()
    total = zb[0].astype(F32)
    for p in range(1, nq):
        total += zb[p].astype(F32)
    adjoint(gain_ref, parts, hats, rstds, gl, (total * scale).astype(BF16), out_ref)

    for copy in sent:
        copy.wait_send()
    for o in range(nq):
        g2 = lax.rem(g + nq - o, nq)

        @pl.when(g2 != q)
        def _():
            send(allr.at[h, g2], rt.at[h, q], ps.at[o], pr.at[q], (g2, me)).wait_send()

        tile = lax.rem(q + nq - o, nq)

        @pl.when(tile != g)
        def _():
            send(sums.at[o], zb.at[g], gzs.at[o], gzr.at[g], (q, 2 * tile + h)).wait_send()


def local(
    homolog_features,
    standardize_scale,
    left_factor_matrix,
    right_factor_matrix,
    final_mapping_matrix,
    final_offset_entries,
    incoming_sensitivity,
):
    seqs, residues, feats = homolog_features.shape
    chan = left_factor_matrix.shape[1]
    zdim = final_mapping_matrix.shape[1]
    cols = incoming_sensitivity.shape[1]
    nq = lax.axis_size("seq")
    wide = residues * chan

    def sds(*shape):
        return jax.ShapeDtypeStruct(shape, BF16)

    one = VMEM((seqs, wide), BF16)
    block = VMEM((nq, seqs, wide), BF16)
    both = VMEM((2, nq, seqs, wide), BF16)
    half = cols * chan // 2
    pair, out = pl.pallas_call(
        functools.partial(kernel, nq, chan),
        out_shape=[sds(residues * cols, zdim), sds(seqs, residues * feats)],
        in_specs=[pl.BlockSpec(memory_space=pltpu.HBM)] * 7,
        out_specs=[pl.BlockSpec(memory_space=VMEM)] * 2,
        scratch_shapes=[
            VMEM((nq, seqs, wide), F32),
            VMEM((seqs * residues, feats), BF16),
            VMEM((1, feats), F32),
            VMEM((chan, feats), BF16),
            VMEM((chan, feats), BF16),
            VMEM((chan * chan, zdim), BF16),
            VMEM((1, zdim), F32),
            VMEM((residues * cols, zdim), BF16),
            VMEM((4, feats, 8 * chan), BF16),
            VMEM((feats // 128 * seqs * residues, 128), F32),
            VMEM((seqs, residues * feats), F32),
            VMEM((residues, seqs, 1), F32),
            one,
            one,
            one,
            block,
            both,
            both,
            VMEM((nq, cols // 4 * residues, 4 * zdim), BF16),
            VMEM((residues * cols, zdim), F32),
            VMEM((2, wide, half), BF16),
            VMEM((nq, 2, wide, half), BF16),
        ]
        + [block] * 4
        + [pltpu.SemaphoreType.DMA((nq,))] * 16
        + [pltpu.SemaphoreType.DMA((7,))],
        compiler_params=pltpu.CompilerParams(
            vmem_limit_bytes=LIMIT, collective_id=0, has_side_effects=True
        ),
        name="outer_mean",
    )(
        homolog_features.reshape(seqs * residues, feats),
        standardize_scale.reshape(1, feats),
        jnp.transpose(left_factor_matrix),
        jnp.transpose(right_factor_matrix),
        final_mapping_matrix,
        final_offset_entries.reshape(1, zdim),
        incoming_sensitivity.reshape(residues * cols, zdim),
    )
    return pair.reshape(residues, cols, zdim), out.reshape(seqs, residues, feats)


def solution(mesh):
    placed = (P("seq", "res", None), P(), P(), P(), P(), P(), P("res", "seq", None))
    return jax.shard_map(
        local,
        mesh=mesh,
        in_specs=placed,
        out_specs=(P("res", "seq", None), P("seq", "res", None)),
        check_vma=False,
    )
```
